128 devices in a mesh: section: 8 (over x, core), ctx: 16 (over y, z).
Axes of the slice: x: 4, y: 4, z: 4, core: 2. Of those that a mesh axis runs over, the one named last changes fastest.
Arguments:
- tokens: bfloat16 [24576, 8192], P(('section', 'ctx')), may hold values from -60 to 60
- norm_gain: float32 [1, 2, 8192], replicated, may hold values from 0.1 to 1.9
- feat_taps: float32 [1, 2, 3, 3, 8192], replicated, may hold values from -3.5 to 3.5
- se_taps: float32 [1, 7, 8192], replicated, may hold values from -2 to 2
- mr_taps: bfloat16 [1, 128, 512], replicated, may hold values from -0.5 to 0.5
Outputs:
- final: bfloat16 [24576, 8192], P(('section', 'ctx'))
The draws below stay inside these ranges and needn't reach their ends.
All inputs are finite; a program needn't handle non-finite values.
Results may differ from the reference program's by a relative error of at most 0.0089.
Values may be sent and summed in bfloat16 or wider, within the bound.
No kernel may reach another device: no remote copies, remote signals or barrier semaphores. Data moves between devices by JAX's collectives and lax.ppermute only.
A program may use at most 192 MiB of HBM per device.

```python
import jax
import jax.numpy as jnp
from jax import lax

D = 8192
GROUPS = 512
FEAT = 3
SE_TAPS = 7
MR_TAPS = 128
LAYERS = 1
SEQ = 24576


def draw_tokens(key, part):
    key_base, key_rows, key_cols = jax.random.split(key, 3)
    base = jax.random.truncated_normal(key_base, -6.0, 6.0, (SEQ, D), jnp.float32)
    row_scale = jnp.exp(jax.random.uniform(key_rows, (SEQ, 1), jnp.float32, -1.15, 1.15))
    col_scale = jnp.exp(jax.random.uniform(key_cols, (1, D), jnp.float32, -1.15, 1.15))
    return (base * row_scale * col_scale).astype(jnp.bfloat16)


def noise(own_key, shape, spread, limit, held_as=jnp.bfloat16):
    return jnp.clip(spread * jax.random.normal(own_key, shape, jnp.float32), -limit, limit).astype(held_as)


def setup_inputs(seed: int = 0) -> dict:
    keys = jax.random.split(jax.random.key(seed), 6)
    tokens = draw_tokens(jax.random.fold_in(keys[5], 71), 0)
    norm_gain = jnp.clip(1.0 + 0.18 * jax.random.normal(keys[1], (LAYERS, 2, D), jnp.float32), 0.1, 1.9)
    feat_taps = noise(keys[2], (LAYERS, 2, 3, FEAT, D), FEAT ** -0.5, 3.5, jnp.float32)
    se_taps = noise(keys[3], (LAYERS, SE_TAPS, D), SE_TAPS ** -0.5, 2.0, jnp.float32)
    mr_taps = noise(keys[4], (LAYERS, MR_TAPS, GROUPS), MR_TAPS ** -0.5, 0.5)
    return {"tokens": tokens, "norm_gain": norm_gain, "feat_taps": feat_taps, "se_taps": se_taps, "mr_taps": mr_taps}


def normalize(hidden, gain):
    values = hidden.astype(jnp.float32)
    mean_square = lax.optimization_barrier(jnp.mean(values * values, axis=-1, keepdims=True))
    return values * lax.rsqrt(mean_square + 1e-06) * gain

def delay(values, lag_rows):
    return jnp.pad(values, ((lag_rows, 0), (0, 0)))[:values.shape[0]]

def short_filter(product, filter_taps):
    values = product.astype(jnp.float32)
    summed = filter_taps[0] * values
    for i in range(1, filter_taps.shape[0]):
        summed = summed + filter_taps[i] * delay(values, i)
    return summed

def long_filter(product, filter_taps):
    values = product.astype(jnp.float32)
    row_total = values.shape[0]
    tap_count = filter_taps.shape[0]
    factor = values.shape[1] // filter_taps.shape[1]
    full_taps = jnp.repeat(filter_taps.astype(jnp.float32), factor, axis=1)
    padded = jnp.pad(values, ((tap_count - 1, 0), (0, 0)))

    def accumulate(i, summed):
        window_rows = lax.dynamic_slice_in_dim(padded, tap_count - 1 - i, row_total, 0)
        tap_row = lax.dynamic_index_in_dim(full_taps, i, 0, keepdims=False)
        return summed + tap_row * window_rows
    return lax.fori_loop(0, tap_count, accumulate, jnp.zeros(values.shape, jnp.float32))

def apply_operator(hidden, gain, feature_taps, filter_fn):
    scaled = normalize(hidden, gain)
    streams = []
    for j in range(3):
        summed = feature_taps[j, 0] * scaled
        for i in range(1, feature_taps.shape[1]):
            summed = summed + feature_taps[j, i] * delay(scaled, i)
        streams.append(summed)
    product = (streams[1] * streams[2]).astype(jnp.bfloat16)
    filtered = filter_fn(product)
    return (hidden.astype(jnp.float32) + streams[0] * filtered).astype(jnp.bfloat16)

def reference(tokens, norm_gain, feat_taps, se_taps, mr_taps):
    hidden = tokens
    for layer in range(LAYERS):
        short_taps = se_taps[layer]
        long_taps = mr_taps[layer]
        hidden = apply_operator(hidden, norm_gain[layer, 0], feat_taps[layer, 0], lambda p: short_filter(p, short_taps))
        hidden = apply_operator(hidden, norm_gain[layer, 1], feat_taps[layer, 1], lambda p: long_filter(p, long_taps))
    return hidden
```

```python
import functools

import jax
import jax.numpy as jnp
import numpy as np
from jax import lax
from jax.experimental import pallas as pl
from jax.experimental.pallas import tpu as pltpu
from jax.sharding import PartitionSpec as P

F32 = jnp.float32
BF16 = jnp.bfloat16
EDGE = 16
HALO = 144
REACH = 128
POINTS = 256
PAD = 8
LANES = 128
WIDE = 256
STEP = 16
EPS = 1e-06
CHUNKS = ((0, 6144), (6144, 2048))
VMEM_LIMIT = 48 * 1024 * 1024


def transform_tables():
    k = np.arange(POINTS // 2)[:, None]
    n = np.arange(POINTS)[None, :]
    angle = np.pi * ((2 * k + 1) * n % (2 * POINTS)) / POINTS
    forward = np.concatenate([np.cos(angle), -np.sin(angle)], axis=0)
    backward = forward.T * (2.0 / POINTS)
    return jnp.asarray(forward, BF16), jnp.asarray(backward, BF16)


def params(vmem=VMEM_LIMIT):
    return pltpu.CompilerParams(vmem_limit_bytes=vmem)


def tap_rows(gain, feat_ref, lanes):
    return [
        [feat_ref[0, 0, j, i : i + 1, lanes] * gain for i in range(3)] for j in range(3)
    ]


def three_taps(scaled_ref, at, taps):
    summed = taps[0] * scaled_ref[pl.ds(at, STEP), :]
    for i in range(1, 3):
        summed = summed + taps[i] * scaled_ref[pl.ds(at - i, STEP), :]
    return summed


def se_filter(product_ref, at, taps):
    summed = taps[0] * product_ref[pl.ds(at, STEP), :]
    for i in range(1, len(taps)):
        summed = summed + taps[i] * product_ref[pl.ds(at - i, STEP), :]
    return summed


def to_row(column, width):
    rows = column.shape[0]
    on = lax.broadcasted_iota(jnp.int32, (rows, width), 0) == lax.broadcasted_iota(
        jnp.int32, (rows, width), 1
    )
    return jnp.sum(jnp.where(on, column, 0.0), axis=0, keepdims=True)


def to_column(row, start, rows):
    width = row.shape[1]
    on = lax.broadcasted_iota(jnp.int32, (rows, width), 0) + start == lax.broadcasted_iota(
        jnp.int32, (rows, width), 1
    )
    return jnp.sum(jnp.where(on, row, 0.0), axis=1, keepdims=True)


def taps_transform_kernel(taps_ref, forward_ref, out_ref):
    wide = out_ref.shape[1]
    groups = taps_ref.shape[1]
    channels = lax.broadcasted_iota(jnp.int32, (groups, wide), 1)
    channels = channels + pl.program_id(0) * wide
    group = lax.broadcasted_iota(jnp.int32, (groups, wide), 0)
    spread = jnp.where((channels >= group * 16) & (channels < group * 16 + 16), 1.0, 0.0)
    full = jnp.dot(taps_ref[...], spread.astype(BF16), preferred_element_type=F32)
    out_ref[...] = jnp.dot(
        forward_ref[...], full.astype(BF16), preferred_element_type=F32
    ).astype(BF16)


def own_se_kernel(
    tokens_ref, edge_ref, gain_ref, feat_ref, se_ref,
    mid_ref, inv_ref, stat_ref,
    first_inv, square, scaled, product,
):
    rows, width = tokens_ref.shape
    total = rows + EDGE
    tiles = width // LANES

    def lanes_of(j):
        return pl.ds(pl.multiple_of(j * LANES, LANES), LANES)

    def read(at, lanes):
        if at < EDGE:
            return edge_ref[at : at + STEP, lanes].astype(F32)
        return tokens_ref[at - EDGE : at - EDGE + STEP, lanes].astype(F32)

    square[...] = jnp.zeros_like(square)

    def add_squares(j, carry):
        lanes = lanes_of(j)
        for at in range(0, total, STEP):
            x = read(at, lanes)
            square[at : at + STEP, :] += x * x
        return carry

    lax.fori_loop(0, tiles, add_squares, 0)
    first = lax.rsqrt(jnp.sum(square[...], axis=1, keepdims=True) / width + EPS)
    first_inv[...] = jnp.broadcast_to(first, first_inv.shape)
    square[...] = jnp.zeros_like(square)
    scaled[0:PAD, :] = jnp.zeros((PAD, LANES), F32)
    product[0:PAD, :] = jnp.zeros((PAD, LANES), F32)

    def one_tile(j, carry):
        lanes = lanes_of(j)
        taps = tap_rows(gain_ref[0, 0:1, lanes], feat_ref, lanes)
        filter_taps = [se_ref[0, i : i + 1, lanes] for i in range(7)]
        for at in range(0, total, STEP):
            x = read(at, lanes)
            scaled[PAD + at : PAD + at + STEP, :] = x * first_inv[at : at + STEP, :]
        for at in range(0, total, STEP):
            k = three_taps(scaled, PAD + at, taps[1])
            v = three_taps(scaled, PAD + at, taps[2])
            product[PAD + at : PAD + at + STEP, :] = (k * v).astype(BF16).astype(F32)
        for at in range(0, total, STEP):
            q = three_taps(scaled, PAD + at, taps[0])
            f = se_filter(product, PAD + at, filter_taps)
            result = (read(at, lanes) + q * f).astype(BF16)
            mid_ref[at : at + STEP, lanes] = result
            wide_result = result.astype(F32)
            square[at : at + STEP, :] += wide_result * wide_result
        return carry

    lax.fori_loop(0, tiles, one_tile, 0)
    second = lax.rsqrt(jnp.sum(square[...], axis=1, keepdims=True) / width + EPS)
    inv_ref[...] = jnp.broadcast_to(second, inv_ref.shape)
    stat_ref[...] = jnp.zeros_like(stat_ref)
    stat_ref[0:1, :] = to_row(first[EDGE:], stat_ref.shape[1])
    stat_ref[1:2, :] = to_row(second[EDGE:], stat_ref.shape[1])


def multiply_spectra(spectrum, taps_ref, out_ref):
    half = POINTS // 2
    for at in range(0, half, STEP):
        a, b = spectrum[at : at + STEP], spectrum[half + at : half + at + STEP]
        c = taps_ref[at : at + STEP, :].astype(F32)
        d = taps_ref[half + at : half + at + STEP, :].astype(F32)
        out_ref[at : at + STEP, :] = (a * c - b * d).astype(BF16)
        out_ref[half + at : half + at + STEP, :] = (a * d + b * c).astype(BF16)


def own_mr_kernel(
    mid_ref, inv_ref, gain_ref, feat_ref, table_ref, forward_ref, backward_ref,
    out_ref, base_ref, gate_ref,
    scaled, product, gate, spectrum, late_spectrum,
):
    total = mid_ref.shape[0]
    rows = total - EDGE
    for half in range(WIDE // LANES):
        lanes = pl.ds(half * LANES, LANES)
        taps = tap_rows(gain_ref[0, 1:2, lanes], feat_ref, lanes)
        for at in range(0, total, STEP):
            scaled[at : at + STEP, :] = (
                mid_ref[at : at + STEP, lanes].astype(F32) * inv_ref[at : at + STEP, :]
            )
        for at in range(0, rows, STEP):
            k = three_taps(scaled, EDGE + at, taps[1])
            v = three_taps(scaled, EDGE + at, taps[2])
            product[at : at + STEP, lanes] = (k * v).astype(BF16)
            gate[at : at + STEP, lanes] = three_taps(scaled, EDGE + at, taps[0])
    early = jnp.dot(
        forward_ref[:, REACH:], product[0:REACH, :], preferred_element_type=F32
    )
    late = jnp.dot(
        forward_ref[:, 0:rows], product[...], preferred_element_type=F32
    )
    multiply_spectra(early, table_ref, spectrum)
    multiply_spectra(late, table_ref, late_spectrum)
    first = jnp.dot(backward_ref[REACH:, :], spectrum[...], preferred_element_type=F32)
    last = jnp.dot(
        backward_ref[REACH:rows, :], late_spectrum[...], preferred_element_type=F32
    )
    for at in range(0, REACH, STEP):
        q = gate[at : at + STEP, :]
        h = mid_ref[EDGE + at : EDGE + at + STEP, :].astype(F32)
        base_ref[at : at + STEP, :] = h + q * first[at : at + STEP]
        gate_ref[at : at + STEP, :] = q
    for at in range(0, rows - REACH, STEP):
        q = gate[REACH + at : REACH + at + STEP, :]
        h = mid_ref[EDGE + REACH + at : EDGE + REACH + at + STEP, :].astype(F32)
        out_ref[at : at + STEP, :] = (h + q * last[at : at + STEP]).astype(BF16)


def halo_kernel(
    main_ref, edge_ref, stat_ref, gain_ref, feat_first_ref, se_ref, feat_ref, table_ref,
    forward_ref, backward_ref, base_ref, gate_ref, held_ref,
    out_ref,
    first_inv, second_inv, scaled, se_product, again, product, spectrum,
):
    del held_ref
    main_rows = main_ref.shape[0]
    own_rows = base_ref.shape[0] + 64

    @pl.when(pl.program_id(0) == 0)
    def _():
        start = own_rows - HALO
        first_inv[...] = jnp.broadcast_to(
            to_column(stat_ref[0:1, :], start, HALO), first_inv.shape
        )
        second_inv[...] = jnp.broadcast_to(
            to_column(stat_ref[1:2, :], start, HALO), second_inv.shape
        )
        scaled[0:PAD, :] = jnp.zeros((PAD, LANES), F32)
        se_product[0:PAD, :] = jnp.zeros((PAD, LANES), F32)

    def read(at, lanes):
        if at < main_rows:
            return main_ref[at : at + STEP, lanes].astype(F32)
        return edge_ref[at - main_rows : at - main_rows + STEP, lanes].astype(F32)

    for half in range(WIDE // LANES):
        lanes = pl.ds(half * LANES, LANES)
        taps = tap_rows(gain_ref[0, 0:1, lanes], feat_first_ref, lanes)
        filter_taps = [se_ref[0, i : i + 1, lanes] for i in range(7)]
        late_taps = tap_rows(gain_ref[0, 1:2, lanes], feat_ref, lanes)
        for at in range(0, HALO, STEP):
            scaled[PAD + at : PAD + at + STEP, :] = (
                read(at, lanes) * first_inv[at : at + STEP, :]
            )
        for at in range(0, HALO, STEP):
            k = three_taps(scaled, PAD + at, taps[1])
            v = three_taps(scaled, PAD + at, taps[2])
            se_product[PAD + at : PAD + at + STEP, :] = (k * v).astype(BF16).astype(F32)
        for at in range(0, HALO, STEP):
            q = three_taps(scaled, PAD + at, taps[0])
            f = se_filter(se_product, PAD + at, filter_taps)
            result = (read(at, lanes) + q * f).astype(BF16).astype(F32)
            again[at : at + STEP, :] = result * second_inv[at : at + STEP, :]
        for at in range(HALO - REACH, HALO, STEP):
            k = three_taps(again, at, late_taps[1])
            v = three_taps(again, at, late_taps[2])
            to = at - (HALO - REACH)
            product[to : to + STEP, lanes] = (k * v).astype(BF16)
    seen = jnp.dot(
        forward_ref[:, 0:REACH], product[...], preferred_element_type=F32
    )
    multiply_spectra(seen, table_ref, spectrum)
    carried = jnp.dot(
        backward_ref[REACH:, :], spectrum[...], preferred_element_type=F32
    )
    for at in range(0, REACH, STEP):
        out_ref[at : at + STEP, :] = (
            base_ref[at : at + STEP, :]
            + gate_ref[at : at + STEP, :] * carried[at : at + STEP]
        ).astype(BF16)


def whole(array):
    return pl.BlockSpec(array.shape, lambda *_: (0,) * array.ndim)


def on_device(tokens, norm_gain, feat_taps, se_taps, mr_taps):
    rows, width = tokens.shape
    total = rows + EDGE
    tiles = width // WIDE
    forward, backward = transform_tables()
    length = lax.axis_size(("section", "ctx"))

    def from_behind(x):
        pairs = [(i, i + 1) for i in range(length - 1)]
        return lax.ppermute(x, ("section", "ctx"), pairs)

    edge = from_behind(tokens[rows - EDGE :])
    mains = [
        from_behind(tokens[rows - HALO : rows - EDGE, start : start + size])
        for start, size in CHUNKS
    ]

    table = pl.pallas_call(
        taps_transform_kernel,
        grid=(width // 1024,),
        in_specs=[
            whole(mr_taps[0]),
            pl.BlockSpec((POINTS, REACH), lambda j: (0, 0)),
        ],
        out_specs=pl.BlockSpec((POINTS, 1024), lambda j: (0, j)),
        out_shape=jax.ShapeDtypeStruct((POINTS, width), BF16),
        compiler_params=params(),
        name="taps_transform",
    )(mr_taps[0], forward)

    mid, inv, stat = pl.pallas_call(
        own_se_kernel,
        grid=(1,),
        in_specs=[
            whole(tokens),
            whole(edge),
            whole(norm_gain),
            pl.BlockSpec((1, 1, 3, 3, width), lambda i: (0, 0, 0, 0, 0)),
            whole(se_taps),
        ],
        out_specs=[
            pl.BlockSpec((total, width), lambda i: (0, 0)),
            pl.BlockSpec((total, LANES), lambda i: (0, 0)),
            pl.BlockSpec((8, WIDE), lambda i: (0, 0)),
        ],
        out_shape=[
            jax.ShapeDtypeStruct((total, width), BF16),
            jax.ShapeDtypeStruct((total, LANES), F32),
            jax.ShapeDtypeStruct((8, WIDE), F32),
        ],
        scratch_shapes=[
            pltpu.VMEM((total, LANES), F32),
            pltpu.VMEM((total, LANES), F32),
            pltpu.VMEM((PAD + total, LANES), F32),
            pltpu.VMEM((PAD + total, LANES), F32),
        ],
        compiler_params=params(),
        name="own_se",
    )(tokens, edge, norm_gain, feat_taps, se_taps)
    halo_stat = from_behind(stat)

    def feat_spec(which, first):
        return pl.BlockSpec((1, 1, 3, 3, WIDE), lambda j: (0, which, 0, 0, first + j))

    out, base, gate = pl.pallas_call(
        own_mr_kernel,
        grid=(tiles,),
        in_specs=[
            pl.BlockSpec((total, WIDE), lambda j: (0, j)),
            whole(inv),
            pl.BlockSpec((1, 2, WIDE), lambda j: (0, 0, j)),
            feat_spec(1, 0),
            pl.BlockSpec((POINTS, WIDE), lambda j: (0, j)),
            whole(forward),
            whole(backward),
        ],
        out_specs=[
            pl.BlockSpec((rows - REACH, WIDE), lambda j: (REACH // (rows - REACH), j)),
            pl.BlockSpec((REACH, WIDE), lambda j: (0, j)),
            pl.BlockSpec((REACH, WIDE), lambda j: (0, j)),
        ],
        out_shape=[
            jax.ShapeDtypeStruct((rows, width), BF16),
            jax.ShapeDtypeStruct((REACH, width), F32),
            jax.ShapeDtypeStruct((REACH, width), F32),
        ],
        scratch_shapes=[
            pltpu.VMEM((total, LANES), F32),
            pltpu.VMEM((rows, WIDE), BF16),
            pltpu.VMEM((rows, WIDE), F32),
            pltpu.VMEM((POINTS, WIDE), BF16),
            pltpu.VMEM((POINTS, WIDE), BF16),
        ],
        compiler_params=params(),
        name="own_mr",
    )(mid, inv, norm_gain, feat_taps, table, forward, backward)

    for (start, size), main in zip(CHUNKS, mains):
        first = start // WIDE
        out = pl.pallas_call(
            halo_kernel,
            grid=(size // WIDE,),
            in_specs=[
                pl.BlockSpec((HALO - EDGE, WIDE), lambda j: (0, j)),
                pl.BlockSpec((EDGE, WIDE), lambda j, f=first: (0, f + j)),
                whole(halo_stat),
                pl.BlockSpec((1, 2, WIDE), lambda j, f=first: (0, 0, f + j)),
                feat_spec(0, first),
                pl.BlockSpec((1, 7, WIDE), lambda j, f=first: (0, 0, f + j)),
                feat_spec(1, first),
                pl.BlockSpec((POINTS, WIDE), lambda j, f=first: (0, f + j)),
                whole(forward),
                whole(backward),
                pl.BlockSpec((REACH, WIDE), lambda j, f=first: (0, f + j)),
                pl.BlockSpec((REACH, WIDE), lambda j, f=first: (0, f + j)),
                pl.BlockSpec(memory_space=pl.ANY),
            ],
            out_specs=pl.BlockSpec((REACH, WIDE), lambda j, f=first: (0, f + j)),
            out_shape=jax.ShapeDtypeStruct((rows, width), BF16),
            input_output_aliases={12: 0},
            scratch_shapes=[
                pltpu.VMEM((HALO, LANES), F32),
                pltpu.VMEM((HALO, LANES), F32),
                pltpu.VMEM((PAD + HALO, LANES), F32),
                pltpu.VMEM((PAD + HALO, LANES), F32),
                pltpu.VMEM((HALO, LANES), F32),
                pltpu.VMEM((REACH, WIDE), BF16),
                pltpu.VMEM((POINTS, WIDE), BF16),
            ],
            compiler_params=params(),
            name="halo",
        )(
            main, edge, halo_stat, norm_gain, feat_taps, se_taps, feat_taps, table,
            forward, backward, base, gate, out,
        )
    return out


def solution(mesh):
    placed = (P(("section", "ctx"), None), P(), P(), P(), P())
    return jax.shard_map(
        on_device,
        mesh=mesh,
        in_specs=placed,
        out_specs=P(("section", "ctx"), None),
        check_vma=False,
    )
```

```python
import functools

import jax
import jax.numpy as jnp
import numpy as np
from jax import lax
from jax.experimental import pallas as pl
from jax.experimental.pallas import tpu as pltpu
from jax.sharding import PartitionSpec as P

F32 = jnp.float32
BF16 = jnp.bfloat16
EDGE = 16
HALO = 144
REACH = 128
POINTS = 256
HEAD = 32
PAD = 8
LANES = 128
WIDE = 256
STEP = 16
EPS = 1e-06
EARLY = (6144, 2048)
LATE = ((0, 2048), (2048, 2048), (4096, 2048))
OWN_BLOCK = 1024
HALO_BLOCK = 512
TAIL_BLOCK = 1024
VMEM_LIMIT = 20 * 1024 * 1024


def transform_tables():
    k = np.arange(POINTS // 2)[:, None]
    n = np.arange(POINTS)[None, :]
    angle = np.pi * ((2 * k + 1) * n % (2 * POINTS)) / POINTS
    forward = np.concatenate([np.cos(angle), -np.sin(angle)], axis=0)
    backward = forward.T * (2.0 / POINTS)
    return jnp.asarray(forward, BF16), jnp.asarray(backward, BF16)


def params(vmem=VMEM_LIMIT):
    return pltpu.CompilerParams(vmem_limit_bytes=vmem)


def cost(micros):
    return pl.CostEstimate(
        flops=int(micros * 1e6), bytes_accessed=int(micros * 3.7e6), transcendentals=0
    )


def tap_rows(gain, feat_ref, lanes):
    return [
        [feat_ref[0, 0, j, i : i + 1, lanes] * gain for i in range(3)] for j in range(3)
    ]


def three_taps(scaled_ref, at, taps):
    summed = taps[0] * scaled_ref[pl.ds(at, STEP), :]
    for i in range(1, 3):
        summed = summed + taps[i] * scaled_ref[pl.ds(at - i, STEP), :]
    return summed


def se_filter(product_ref, at, taps):
    summed = taps[0] * product_ref[pl.ds(at, STEP), :]
    for i in range(1, len(taps)):
        summed = summed + taps[i] * product_ref[pl.ds(at - i, STEP), :]
    return summed


def to_row(column, width):
    rows = column.shape[0]
    on = lax.broadcasted_iota(jnp.int32, (rows, width), 0) == lax.broadcasted_iota(
        jnp.int32, (rows, width), 1
    )
    return jnp.sum(jnp.where(on, column, 0.0), axis=0, keepdims=True)


def to_column(row, start, rows):
    width = row.shape[1]
    on = lax.broadcasted_iota(jnp.int32, (rows, width), 0) + start == lax.broadcasted_iota(
        jnp.int32, (rows, width), 1
    )
    return jnp.sum(jnp.where(on, row, 0.0), axis=1, keepdims=True)


def first_block():
    return (lax.axis_index("section") == 0) & (lax.axis_index("ctx") == 0)


def taps_transform_kernel(taps_ref, forward_ref, out_ref, spread):
    groups, wide = spread.shape

    @pl.when(pl.program_id(0) == 0)
    def _():
        channel = lax.broadcasted_iota(jnp.int32, (groups, wide), 1)
        group = lax.broadcasted_iota(jnp.int32, (groups, wide), 0)
        inside = (channel >= group * 16) & (channel < group * 16 + 16)
        spread[...] = jnp.where(inside, 1.0, 0.0).astype(BF16)

    few = jnp.dot(
        forward_ref[...], taps_ref[...], preferred_element_type=F32
    ).astype(BF16)
    for at in range(0, wide, WIDE):
        out_ref[:, at : at + WIDE] = jnp.dot(
            few, spread[:, at : at + WIDE], preferred_element_type=F32
        ).astype(BF16)


def lanes_of(j):
    return pl.ds(pl.multiple_of(j * LANES, LANES), LANES)


def se_operator(
    read, rows, first_row, width, shown, gain_ref, feat_ref, se_ref,
    mid_ref, first_inv, square, scaled, product,
):
    tiles = width // LANES
    square[...] = jnp.zeros_like(square)

    def add_squares(j, carry):
        for at in range(0, rows, STEP):
            summed = square[at : at + STEP, :]
            for i in range(8):
                x = read(at, j * 8 + i)
                summed = summed + x * x
            square[at : at + STEP, :] = summed
        return carry

    lax.fori_loop(0, tiles // 8, add_squares, 0)
    first = lax.rsqrt(jnp.sum(square[...], axis=1, keepdims=True) / width + EPS)
    first_inv[...] = jnp.broadcast_to(first, first_inv.shape)
    if shown is not None:
        first_inv[0:EDGE, :] = first_inv[0:EDGE, :] * shown
    square[...] = jnp.zeros_like(square)
    scaled[0:PAD, :] = jnp.zeros((PAD, LANES), F32)
    product[0:PAD, :] = jnp.zeros((PAD, LANES), F32)

    def one_tile(j, carry):
        lanes = lanes_of(j)
        taps = tap_rows(gain_ref[0, 0:1, lanes], feat_ref, lanes)
        filter_taps = [se_ref[0, i : i + 1, lanes] for i in range(7)]
        for at in range(0, rows, STEP):
            x = read(at, j)
            scaled[PAD + at : PAD + at + STEP, :] = x * first_inv[at : at + STEP, :]
        for at in range(0, rows, STEP):
            k = three_taps(scaled, PAD + at, taps[1])
            v = three_taps(scaled, PAD + at, taps[2])
            product[PAD + at : PAD + at + STEP, :] = (k * v).astype(BF16).astype(F32)
        for at in range(first_row, rows, STEP):
            q = three_taps(scaled, PAD + at, taps[0])
            f = se_filter(product, PAD + at, filter_taps)
            result = (read(at, j) + q * f).astype(BF16)
            mid_ref[at - first_row : at - first_row + STEP, lanes] = result
            wide_result = result.astype(F32)
            square[at : at + STEP, :] += wide_result * wide_result
        return carry

    lax.fori_loop(0, tiles, one_tile, 0)
    second = lax.rsqrt(
        jnp.sum(square[first_row:, :], axis=1, keepdims=True) / width + EPS
    )
    return first, second


def own_se_kernel(
    tokens_ref, gain_ref, feat_ref, se_ref, late_feat_ref,
    mid_ref, inv_ref, *rest,
):
    rows, width = tokens_ref.shape
    tail_refs, scratch = rest[: len(LATE)], rest[len(LATE) :]
    scaled = scratch[2]

    def read(at, j):
        return tokens_ref[at : at + STEP, lanes_of(j)].astype(F32)

    first, second = se_operator(
        read, rows, EDGE, width, None, gain_ref, feat_ref, se_ref, mid_ref, *scratch
    )
    inv_ref[...] = jnp.broadcast_to(second, inv_ref.shape)
    lead = rows - HALO

    for (start, size), tail_ref in zip(LATE, tail_refs):

        def one_tail(j, carry, start=start, tail_ref=tail_ref):
            lanes = lanes_of(start // LANES + j)
            taps = tap_rows(gain_ref[0, 1:2, lanes], late_feat_ref, lanes)
            for at in range(0, HALO, STEP):
                own = lead - EDGE + at
                scaled[at : at + STEP, :] = (
                    mid_ref[own : own + STEP, lanes].astype(F32)
                    * inv_ref[own : own + STEP, :]
                )
            for at in range(HALO - REACH, HALO, STEP):
                k = three_taps(scaled, at, taps[1])
                v = three_taps(scaled, at, taps[2])
                to = at - (HALO - REACH)
                tail_ref[to : to + STEP, lanes_of(j)] = (k * v).astype(BF16)
            return carry

        lax.fori_loop(0, size // LANES, one_tail, 0)

    top = lax.broadcasted_iota(jnp.int32, (STEP, WIDE), 0) == 0
    for i, norms in enumerate((first[EDGE:], second)):
        left = to_row(norms, WIDE)
        for k in range(3):
            piece = left.astype(BF16).astype(F32)
            left = left - piece
            lanes = pl.ds((i * 3 + k) * WIDE, WIDE)
            rest_of = tail_refs[0][0:STEP, lanes].astype(F32)
            tail_refs[0][0:STEP, lanes] = jnp.where(top, piece, rest_of).astype(BF16)


def head_se_kernel(
    tokens_ref, early_ref, gain_ref, feat_ref, se_ref,
    mid_ref, inv_ref,
    *scratch,
):
    width = tokens_ref.shape[1]
    shown = jnp.where(first_block(), 0.0, 1.0)

    span = EARLY[1] // LANES
    parts = EARLY[0] // EARLY[1]

    def read(at, j):
        if at < EDGE:
            part = lax.div(j, span)
            row = jnp.where(part < parts, HALO + EDGE * part, HALO - EDGE)
            column = j - span * part
            rows = pl.ds(pl.multiple_of(row + at, STEP), STEP)
            return early_ref[rows, lanes_of(column)].astype(F32)
        return tokens_ref[at - EDGE : at - EDGE + STEP, lanes_of(j)].astype(F32)

    _, second = se_operator(
        read, HEAD, 0, width, shown, gain_ref, feat_ref, se_ref, mid_ref, *scratch
    )
    inv_ref[...] = jnp.broadcast_to(second, inv_ref.shape)
    inv_ref[0:EDGE, :] = inv_ref[0:EDGE, :] * shown


def multiply_spectra(spectrum, taps_ref, out_ref, lanes):
    half = POINTS // 2
    for at in range(0, half, STEP):
        a, b = spectrum[at : at + STEP], spectrum[half + at : half + at + STEP]
        c = taps_ref[at : at + STEP, lanes].astype(F32)
        d = taps_ref[half + at : half + at + STEP, lanes].astype(F32)
        out_ref[at : at + STEP, lanes] = (a * c - b * d).astype(BF16)
        out_ref[half + at : half + at + STEP, lanes] = (a * d + b * c).astype(BF16)


def staggered(count, *stages):
    for step in range(count + len(stages) - 1):
        for i, stage in enumerate(stages):
            if 0 <= step - i < count:
                stage(step - i)


def own_mr_kernel(
    head_ref, mid_ref, head_inv_ref, inv_ref, gain_ref, feat_ref, table_ref,
    forward_ref, backward_ref,
    out_ref, base_ref, gate_ref,
    scaled, product, late_gate, spectrum, late_spectrum,
):
    total = HEAD + mid_ref.shape[0]
    rows = total - EDGE

    def read(at, lanes):
        if at < HEAD:
            return head_ref[at : at + STEP, lanes].astype(F32)
        return mid_ref[at - HEAD : at - HEAD + STEP, lanes].astype(F32)

    def inverse(at):
        if at < HEAD:
            return head_inv_ref[at : at + STEP, :]
        return inv_ref[at - HEAD : at - HEAD + STEP, :]

    def streams(tile):
        for half in range(WIDE // LANES):
            lanes = pl.ds(tile * WIDE + half * LANES, LANES)
            column = scaled.at[tile * 2 + half]
            taps = tap_rows(gain_ref[0, 1:2, lanes], feat_ref, lanes)
            for at in range(0, total, STEP):
                column[at : at + STEP, :] = read(at, lanes) * inverse(at)
            for at in range(0, rows, STEP):
                k = three_taps(column, EDGE + at, taps[1])
                v = three_taps(column, EDGE + at, taps[2])
                w = (k * v).astype(BF16)
                product[at : at + STEP, lanes] = w
                q = three_taps(column, EDGE + at, taps[0])
                if at < REACH:
                    gate_ref[at : at + STEP, lanes] = q
                else:
                    late_gate[at - REACH : at - REACH + STEP, lanes] = q

    def spectra(tile):
        lanes = pl.ds(tile * WIDE, WIDE)
        early = jnp.dot(
            forward_ref[:, REACH:], product[0:REACH, lanes], preferred_element_type=F32
        )
        multiply_spectra(early, table_ref, spectrum, lanes)
        late = jnp.dot(
            forward_ref[:, 0:rows], product[:, lanes], preferred_element_type=F32
        )
        multiply_spectra(late, table_ref, late_spectrum, lanes)

    def results(tile):
        lanes = pl.ds(tile * WIDE, WIDE)
        first = jnp.dot(
            backward_ref[REACH:, :], spectrum[:, lanes], preferred_element_type=F32
        )
        for at in range(0, REACH, STEP):
            base_ref[at : at + STEP, lanes] = (
                read(EDGE + at, lanes)
                + gate_ref[at : at + STEP, lanes] * first[at : at + STEP]
            )
        last = jnp.dot(
            backward_ref[REACH:rows, :],
            late_spectrum[:, lanes],
            preferred_element_type=F32,
        )
        for at in range(0, rows - REACH, STEP):
            out_ref[at : at + STEP, lanes] = (
                read(EDGE + REACH + at, lanes)
                + late_gate[at : at + STEP, lanes] * last[at : at + STEP]
            ).astype(BF16)

    staggered(mid_ref.shape[1] // WIDE, streams, spectra, results)


def halo_kernel(
    main_ref, stat_ref, gain_ref, feat_first_ref, se_ref, feat_ref, table_ref,
    forward_ref, backward_ref, base_ref, gate_ref, held_ref,
    out_ref,
    first_inv, second_inv, scaled, se_product, again, product, spectrum,
    *, start,
):
    del held_ref
    columns = scaled.shape[0]

    @pl.when(pl.program_id(0) == 0)
    def _():
        shown = jnp.where(first_block(), 0.0, 1.0)
        for i, inverse in enumerate((first_inv, second_inv)):
            row = jnp.zeros((1, WIDE), F32)
            for k in range(3):
                lanes = pl.ds((i * 3 + k) * WIDE, WIDE)
                row = row + stat_ref[0:STEP, lanes].astype(F32)[0:1]
            column = to_column(row * shown, start, HALO)
            inverse[...] = jnp.broadcast_to(column, inverse.shape)
        scaled[:, 0:PAD, :] = jnp.zeros((columns, PAD, LANES), F32)
        se_product[:, 0:PAD, :] = jnp.zeros((columns, PAD, LANES), F32)

    def read(at, lanes):
        return main_ref[at : at + STEP, lanes].astype(F32)

    def streams(tile):
        for half in range(WIDE // LANES):
            lanes = pl.ds(tile * WIDE + half * LANES, LANES)
            column = scaled.at[tile * 2 + half]
            se_column = se_product.at[tile * 2 + half]
            late_column = again.at[tile * 2 + half]
            taps = tap_rows(gain_ref[0, 0:1, lanes], feat_first_ref, lanes)
            filter_taps = [se_ref[0, i : i + 1, lanes] for i in range(7)]
            late_taps = tap_rows(gain_ref[0, 1:2, lanes], feat_ref, lanes)
            for at in range(0, HALO, STEP):
                column[PAD + at : PAD + at + STEP, :] = (
                    read(at, lanes) * first_inv[at : at + STEP, :]
                )
            for at in range(0, HALO, STEP):
                k = three_taps(column, PAD + at, taps[1])
                v = three_taps(column, PAD + at, taps[2])
                se_column[PAD + at : PAD + at + STEP, :] = (
                    (k * v).astype(BF16).astype(F32)
                )
            for at in range(0, HALO, STEP):
                q = three_taps(column, PAD + at, taps[0])
                f = se_filter(se_column, PAD + at, filter_taps)
                result = (read(at, lanes) + q * f).astype(BF16).astype(F32)
                late_column[at : at + STEP, :] = result * second_inv[at : at + STEP, :]
            for at in range(HALO - REACH, HALO, STEP):
                k = three_taps(late_column, at, late_taps[1])
                v = three_taps(late_column, at, late_taps[2])
                to = at - (HALO - REACH)
                product[to : to + STEP, lanes] = (k * v).astype(BF16)

    def spectra(tile):
        halo_spectra(tile, product, forward_ref, table_ref, spectrum)

    def results(tile):
        halo_results(tile, spectrum, backward_ref, base_ref, gate_ref, out_ref)

    staggered(main_ref.shape[1] // WIDE, streams, spectra, results)


def halo_spectra(tile, product, forward_ref, table_ref, spectrum):
    lanes = pl.ds(tile * WIDE, WIDE)
    seen = jnp.dot(
        forward_ref[:, 0:REACH], product[:, lanes], preferred_element_type=F32
    )
    multiply_spectra(seen, table_ref, spectrum, lanes)


def halo_results(tile, spectrum, backward_ref, base_ref, gate_ref, out_ref):
    lanes = pl.ds(tile * WIDE, WIDE)
    carried = jnp.dot(
        backward_ref[REACH:, :], spectrum[:, lanes], preferred_element_type=F32
    )
    for at in range(0, REACH, STEP):
        out_ref[at : at + STEP, lanes] = (
            base_ref[at : at + STEP, lanes]
            + gate_ref[at : at + STEP, lanes] * carried[at : at + STEP]
        ).astype(BF16)


def tail_kernel(
    tail_ref, shown_table_ref, forward_ref, backward_ref, base_ref, gate_ref, held_ref,
    out_ref,
    product, spectrum,
):
    del held_ref
    shown = jnp.where(first_block(), 0.0, 1.0)
    block = tail_ref.shape[1]

    def arrived(tile):
        lanes = pl.ds(tile * WIDE, WIDE)
        for at in range(0, REACH, STEP):
            w = tail_ref[at : at + STEP, lanes].astype(F32) * shown
            if at == 0:
                w = jnp.where(
                    lax.broadcasted_iota(jnp.int32, w.shape, 0) == 0, 0.0, w
                )
            product[at : at + STEP, lanes] = w.astype(BF16)

    def spectra(tile):
        halo_spectra(tile, product, forward_ref, shown_table_ref, spectrum)

    def results(tile):
        halo_results(tile, spectrum, backward_ref, base_ref, gate_ref, out_ref)

    staggered(block // WIDE, arrived, spectra, results)


def whole(array):
    return pl.BlockSpec(array.shape, lambda *_: (0,) * array.ndim)


def on_device(tokens, norm_gain, feat_taps, se_taps, mr_taps):
    rows, width = tokens.shape
    total = rows + EDGE
    forward, backward = transform_tables()
    length = lax.axis_size(("section", "ctx"))

    def from_behind(x):
        pairs = [(i, (i + 1) % length) for i in range(length)]
        return lax.ppermute(x, ("section", "ctx"), pairs)

    start, size = EARLY
    early = from_behind(
        jnp.concatenate(
            [tokens[rows - HALO :, start:]]
            + [tokens[rows - EDGE :, i : i + size] for i in range(0, start, size)],
            axis=0,
        )
    )

    groups = 2048 // 16
    table = pl.pallas_call(
        taps_transform_kernel,
        grid=(width // 2048,),
        in_specs=[
            pl.BlockSpec((REACH, groups), lambda j: (0, j)),
            pl.BlockSpec((POINTS, REACH), lambda j: (0, 0)),
        ],
        out_specs=pl.BlockSpec((POINTS, 2048), lambda j: (0, j)),
        out_shape=jax.ShapeDtypeStruct((POINTS, width), BF16),
        scratch_shapes=[pltpu.VMEM((groups, 2048), BF16)],
        compiler_params=params(),
        cost_estimate=cost(2.5),
        name="taps_transform",
    )(mr_taps[0], forward)

    se_specs = [
        whole(norm_gain),
        pl.BlockSpec((1, 1, 3, 3, width), lambda i: (0, 0, 0, 0, 0)),
        whole(se_taps),
    ]

    def se_scratch(height):
        return [
            pltpu.VMEM((height, LANES), F32),
            pltpu.VMEM((height, LANES), F32),
            pltpu.VMEM((PAD + height, LANES), F32),
            pltpu.VMEM((PAD + height, LANES), F32),
        ]

    def all_of(*shape):
        return pl.BlockSpec(shape, lambda *_: (0,) * len(shape))

    mid_rows = rows - EDGE
    mid, inv, *tails = pl.pallas_call(
        own_se_kernel,
        grid=(1,),
        in_specs=[
            whole(tokens),
            *se_specs,
            pl.BlockSpec((1, 1, 3, 3, width), lambda i: (0, 1, 0, 0, 0)),
        ],
        out_specs=[all_of(mid_rows, width), all_of(mid_rows, LANES)]
        + [all_of(REACH, size) for _, size in LATE],
        out_shape=[
            jax.ShapeDtypeStruct((mid_rows, width), BF16),
            jax.ShapeDtypeStruct((mid_rows, LANES), F32),
        ]
        + [jax.ShapeDtypeStruct((REACH, size), BF16) for _, size in LATE],
        scratch_shapes=se_scratch(rows),
        compiler_params=params(),
        cost_estimate=cost(14),
        name="own_se",
    )(tokens, norm_gain, feat_taps, se_taps, feat_taps)
    tails = [from_behind(tail) for tail in tails]

    head, head_inv = pl.pallas_call(
        head_se_kernel,
        grid=(1,),
        in_specs=[all_of(EDGE, width), whole(early), *se_specs],
        out_specs=[all_of(HEAD, width), all_of(HEAD, LANES)],
        out_shape=[
            jax.ShapeDtypeStruct((HEAD, width), BF16),
            jax.ShapeDtypeStruct((HEAD, LANES), F32),
        ],
        scratch_shapes=se_scratch(HEAD),
        compiler_params=params(),
        cost_estimate=cost(3),
        name="head_se",
    )(tokens, early, norm_gain, feat_taps, se_taps)

    def feat_spec(block, which, first):
        return pl.BlockSpec((1, 1, 3, 3, block), lambda j: (0, which, 0, 0, first + j))

    def columns(height, block, first=0, row=0):
        return pl.BlockSpec((height, block), lambda j: (row, first + j))

    block = OWN_BLOCK
    out, base, gate = pl.pallas_call(
        own_mr_kernel,
        grid=(width // block,),
        in_specs=[
            columns(HEAD, block),
            columns(mid_rows, block),
            whole(head_inv),
            whole(inv),
            pl.BlockSpec((1, 2, block), lambda j: (0, 0, j)),
            feat_spec(block, 1, 0),
            columns(POINTS, block),
            whole(forward),
            whole(backward),
        ],
        out_specs=[
            columns(rows - REACH, block, 0, REACH // (rows - REACH)),
            columns(REACH, block),
            columns(REACH, block),
        ],
        out_shape=[
            jax.ShapeDtypeStruct((rows, width), BF16),
            jax.ShapeDtypeStruct((REACH, width), F32),
            jax.ShapeDtypeStruct((REACH, width), F32),
        ],
        scratch_shapes=[
            pltpu.VMEM((block // LANES, rows + EDGE, LANES), F32),
            pltpu.VMEM((rows, block), BF16),
            pltpu.VMEM((rows - REACH, block), F32),
            pltpu.VMEM((POINTS, block), BF16),
            pltpu.VMEM((POINTS, block), BF16),
        ],
        compiler_params=params(),
        cost_estimate=cost(12),
        name="own_mr",
    )(head, mid, head_inv, inv, norm_gain, feat_taps, table, forward, backward)

    block = HALO_BLOCK
    first = start // block
    out = pl.pallas_call(
        functools.partial(halo_kernel, start=mid_rows - HALO),
        grid=(size // block,),
        in_specs=[
            columns(HALO, block),
            all_of(STEP, 6 * WIDE),
            pl.BlockSpec((1, 2, block), lambda j: (0, 0, first + j)),
            feat_spec(block, 0, first),
            pl.BlockSpec((1, 7, block), lambda j: (0, 0, first + j)),
            feat_spec(block, 1, first),
            columns(POINTS, block, first),
            whole(forward),
            whole(backward),
            columns(REACH, block, first),
            columns(REACH, block, first),
            pl.BlockSpec(memory_space=pl.ANY),
        ],
        out_specs=columns(REACH, block, first),
        out_shape=jax.ShapeDtypeStruct((rows, width), BF16),
        input_output_aliases={11: 0},
        scratch_shapes=[
            pltpu.VMEM((HALO, LANES), F32),
            pltpu.VMEM((HALO, LANES), F32),
            pltpu.VMEM((block // LANES, PAD + HALO, LANES), F32),
            pltpu.VMEM((block // LANES, PAD + HALO, LANES), F32),
            pltpu.VMEM((block // LANES, HALO, LANES), F32),
            pltpu.VMEM((REACH, block), BF16),
            pltpu.VMEM((POINTS, block), BF16),
        ],
        compiler_params=params(),
        cost_estimate=cost(6),
        name="halo",
    )(
        early, tails[0], norm_gain, feat_taps, se_taps, feat_taps, table,
        forward, backward, base, gate, out,
    )

    block = TAIL_BLOCK
    for (start, size), tail in zip(LATE, tails):
        out = pl.pallas_call(
            tail_kernel,
            grid=(size // block,),
            in_specs=[
                columns(REACH, block),
                columns(POINTS, block, start // block),
                whole(forward),
                whole(backward),
                columns(REACH, block, start // block),
                columns(REACH, block, start // block),
                pl.BlockSpec(memory_space=pl.ANY),
            ],
            out_specs=columns(REACH, block, start // block),
            out_shape=jax.ShapeDtypeStruct((rows, width), BF16),
            input_output_aliases={6: 0},
            scratch_shapes=[
                pltpu.VMEM((REACH, block), BF16),
                pltpu.VMEM((POINTS, block), BF16),
            ],
            compiler_params=params(),
            cost_estimate=cost(3),
        name="tail",
        )(tail, table, forward, backward, base, gate, out)
    return out


def solution(mesh):
    placed = (P(("section", "ctx"), None), P(), P(), P(), P())
    return jax.shard_map(
        on_device,
        mesh=mesh,
        in_specs=placed,
        out_specs=P(("section", "ctx"), None),
        check_vma=False,
    )
```

```python
import functools

import jax
import jax.numpy as jnp
import numpy as np
from jax import lax
from jax.experimental import pallas as pl
from jax.experimental.pallas import tpu as pltpu
from jax.sharding import PartitionSpec as P

F32 = jnp.float32
BF16 = jnp.bfloat16
EDGE = 16
HALO = 144
REACH = 128
POINTS = 256
HEAD = 32
PAD = 8
LANES = 128
WIDE = 256
STEP = 16
EPS = 1e-06
EARLY = (7168, 1024)
ROUND = (6144, 1024)
LATE = ((0, 2048), (2048, 2048), (4096, 2048))
RING = 4
PIECES = 2
OWN_BLOCK = 1024
HALO_BLOCK = 512
TAIL_BLOCK = 1024
VMEM_LIMIT = 20 * 1024 * 1024


def transform_tables():
    k = np.arange(POINTS // 2)[:, None]
    n = np.arange(POINTS)[None, :]
    angle = np.pi * ((2 * k + 1) * n % (2 * POINTS)) / POINTS
    forward = np.concatenate([np.cos(angle), -np.sin(angle)], axis=0)
    backward = forward.T * (2.0 / POINTS)
    late = forward[:, :REACH] * (np.arange(REACH) > 0)
    return tuple(jnp.asarray(table, BF16) for table in (forward, backward, late))


def params(vmem=VMEM_LIMIT):
    return pltpu.CompilerParams(vmem_limit_bytes=vmem)


def cost(micros):
    return pl.CostEstimate(
        flops=int(micros * 1e6), bytes_accessed=int(micros * 3.7e6), transcendentals=0
    )


def tap_rows(gain, feat_ref, lanes):
    return [
        [feat_ref[0, 0, j, i : i + 1, lanes] * gain for i in range(3)] for j in range(3)
    ]


def three_taps(scaled_ref, at, taps):
    summed = taps[0] * scaled_ref[pl.ds(at, STEP), :]
    for i in range(1, 3):
        summed = summed + taps[i] * scaled_ref[pl.ds(at - i, STEP), :]
    return summed


def se_filter(product_ref, at, taps):
    summed = taps[0] * product_ref[pl.ds(at, STEP), :]
    for i in range(1, len(taps)):
        summed = summed + taps[i] * product_ref[pl.ds(at - i, STEP), :]
    return summed


def to_row(column, width):
    rows = column.shape[0]
    on = lax.broadcasted_iota(jnp.int32, (rows, width), 0) == lax.broadcasted_iota(
        jnp.int32, (rows, width), 1
    )
    return jnp.sum(jnp.where(on, column, 0.0), axis=0, keepdims=True)


def to_column(row, start, rows):
    width = row.shape[1]
    on = lax.broadcasted_iota(jnp.int32, (rows, width), 0) + start == lax.broadcasted_iota(
        jnp.int32, (rows, width), 1
    )
    return jnp.sum(jnp.where(on, row, 0.0), axis=1, keepdims=True)


def first_block():
    return (lax.axis_index("section") == 0) & (lax.axis_index("ctx") == 0)


def gather_kernel(tokens_ref, early_ref, around_ref, done):
    rows = tokens_ref.shape[0]
    halo, edge = pl.ds(rows - HALO, HALO), pl.ds(rows - EDGE, EDGE)
    start, size = EARLY
    moves = [(tokens_ref.at[halo, pl.ds(*ROUND)], around_ref)]
    moves.append((tokens_ref.at[halo, pl.ds(*EARLY)], early_ref.at[pl.ds(0, HALO), :]))
    for i in range(start // size):
        to = early_ref.at[pl.ds(HALO + EDGE * i, EDGE), :]
        moves.append((tokens_ref.at[edge, pl.ds(i * size, size)], to))
    copies = [
        pltpu.make_async_copy(source, to, done.at[i])
        for i, (source, to) in enumerate(moves)
    ]
    for copy in copies:
        copy.start()
    for copy in copies:
        copy.wait()


def taps_transform_kernel(taps_ref, forward_ref, out_ref, spread):
    groups, wide = spread.shape

    @pl.when(pl.program_id(0) == 0)
    def _():
        channel = lax.broadcasted_iota(jnp.int32, (groups, wide), 1)
        group = lax.broadcasted_iota(jnp.int32, (groups, wide), 0)
        inside = (channel >= group * 16) & (channel < group * 16 + 16)
        spread[...] = jnp.where(inside, 1.0, 0.0).astype(BF16)

    few = jnp.dot(
        forward_ref[...], taps_ref[...], preferred_element_type=F32
    ).astype(BF16)
    for at in range(0, wide, WIDE):
        out_ref[:, at : at + WIDE] = jnp.dot(
            few, spread[:, at : at + WIDE], preferred_element_type=F32
        ).astype(BF16)


def lanes_of(j):
    return pl.ds(pl.multiple_of(j * LANES, LANES), LANES)


def se_operator(
    read, rows, first_row, width, shown, gain_ref, feat_ref, se_ref,
    mid_ref, first_inv, square, scaled, product,
):
    tiles = width // LANES
    square[...] = jnp.zeros_like(square)

    def add_squares(j, carry):
        for at in range(0, rows, STEP):
            summed = square[at : at + STEP, :]
            for i in range(8):
                x = read(at, j * 8 + i)
                summed = summed + x * x
            square[at : at + STEP, :] = summed
        return carry

    lax.fori_loop(0, tiles // 8, add_squares, 0)
    first = lax.rsqrt(jnp.sum(square[...], axis=1, keepdims=True) / width + EPS)
    first_inv[...] = jnp.broadcast_to(first, first_inv.shape)
    if shown is not None:
        first_inv[0:EDGE, :] = first_inv[0:EDGE, :] * shown
    square[...] = jnp.zeros_like(square)
    scaled[:, 0:PAD, :] = jnp.zeros((scaled.shape[0], PAD, LANES), F32)
    product[:, 0:PAD, :] = jnp.zeros((scaled.shape[0], PAD, LANES), F32)

    def one_tile(j, scaled, product):
        lanes = lanes_of(j)
        taps = tap_rows(gain_ref[0, 0:1, lanes], feat_ref, lanes)
        filter_taps = [se_ref[0, i : i + 1, lanes] for i in range(7)]
        for at in range(0, rows, STEP):
            x = read(at, j)
            scaled[PAD + at : PAD + at + STEP, :] = x * first_inv[at : at + STEP, :]
        for at in range(0, rows, STEP):
            k = three_taps(scaled, PAD + at, taps[1])
            v = three_taps(scaled, PAD + at, taps[2])
            product[PAD + at : PAD + at + STEP, :] = (k * v).astype(BF16).astype(F32)
        for at in range(first_row, rows, STEP):
            q = three_taps(scaled, PAD + at, taps[0])
            f = se_filter(product, PAD + at, filter_taps)
            result = read(at, j) + q * f
            mid_ref[at - first_row : at - first_row + STEP, lanes] = result.astype(BF16)
            square[at : at + STEP, :] += result * result

    slots = scaled.shape[0]

    def some_tiles(j, carry):
        for i in range(slots):
            one_tile(j * slots + i, scaled.at[i], product.at[i])
        return carry

    lax.fori_loop(0, tiles // slots, some_tiles, 0)
    second = lax.rsqrt(
        jnp.sum(square[first_row:, :], axis=1, keepdims=True) / width + EPS
    )
    return first, second


def own_se_kernel(
    tokens_ref, gain_ref, feat_ref, se_ref, late_feat_ref,
    mid_ref, inv_ref, *rest,
):
    rows, width = tokens_ref.shape
    tail_refs, scratch = rest[: len(LATE)], rest[len(LATE) :]
    scaled = scratch[2].at[0]

    def read(at, j):
        return tokens_ref[at : at + STEP, lanes_of(j)].astype(F32)

    first, second = se_operator(
        read, rows, EDGE, width, None, gain_ref, feat_ref, se_ref, mid_ref, *scratch
    )
    inv_ref[...] = jnp.broadcast_to(second, inv_ref.shape)
    lead = rows - HALO

    for (start, size), tail_ref in zip(LATE, tail_refs):

        def one_tail(j, carry, start=start, tail_ref=tail_ref):
            lanes = lanes_of(start // LANES + j)
            taps = tap_rows(gain_ref[0, 1:2, lanes], late_feat_ref, lanes)
            for at in range(0, HALO, STEP):
                own = lead - EDGE + at
                scaled[at : at + STEP, :] = (
                    mid_ref[own : own + STEP, lanes].astype(F32)
                    * inv_ref[own : own + STEP, :]
                )
            for at in range(HALO - REACH, HALO, STEP):
                k = three_taps(scaled, at, taps[1])
                v = three_taps(scaled, at, taps[2])
                to = at - (HALO - REACH)
                tail_ref[to : to + STEP, lanes_of(j)] = (k * v).astype(BF16)
            return carry

        lax.fori_loop(0, size // LANES, one_tail, 0)

    top = lax.broadcasted_iota(jnp.int32, (STEP, WIDE), 0) == 0
    for i, norms in enumerate((first[EDGE:], second)):
        left = to_row(norms, WIDE)
        for k in range(PIECES):
            piece = left.astype(BF16).astype(F32)
            left = left - piece
            lanes = pl.ds((i * PIECES + k) * WIDE, WIDE)
            rest_of = tail_refs[0][0:STEP, lanes].astype(F32)
            tail_refs[0][0:STEP, lanes] = jnp.where(top, piece, rest_of).astype(BF16)


def head_se_kernel(
    tokens_ref, early_ref, gain_ref, feat_ref, se_ref,
    mid_ref, inv_ref,
    *scratch,
):
    width = tokens_ref.shape[1]
    shown = jnp.where(first_block(), 0.0, 1.0)

    span = EARLY[1] // LANES
    own_part = EARLY[0] // LANES

    def read(at, j):
        if at < EDGE:
            part = lax.div(j, span)
            row = jnp.where(j < own_part, HALO + EDGE * part, HALO - EDGE)
            column = jnp.where(j < own_part, j - span * part, j - own_part)
            rows = pl.ds(pl.multiple_of(row + at, STEP), STEP)
            return early_ref[rows, lanes_of(column)].astype(F32)
        return tokens_ref[at - EDGE : at - EDGE + STEP, lanes_of(j)].astype(F32)

    _, second = se_operator(
        read, HEAD, 0, width, shown, gain_ref, feat_ref, se_ref, mid_ref, *scratch
    )
    inv_ref[...] = jnp.broadcast_to(second, inv_ref.shape)
    inv_ref[0:EDGE, :] = inv_ref[0:EDGE, :] * shown


def multiply_spectra(spectrum, taps_ref, out_ref, lanes):
    half = POINTS // 2
    for at in range(0, half, STEP):
        a, b = spectrum[at : at + STEP], spectrum[half + at : half + at + STEP]
        c = taps_ref[at : at + STEP, lanes].astype(F32)
        d = taps_ref[half + at : half + at + STEP, lanes].astype(F32)
        out_ref[at : at + STEP, lanes] = (a * c - b * d).astype(BF16)
        out_ref[half + at : half + at + STEP, lanes] = (a * d + b * c).astype(BF16)


def staggered(count, *stages):
    for step in range(count + len(stages) - 1):
        for i, stage in enumerate(stages):
            if 0 <= step - i < count:
                stage(step - i)


def own_mr_kernel(
    head_ref, mid_ref, head_inv_ref, inv_ref, gain_ref, feat_ref, table_ref,
    forward_ref, backward_ref,
    out_ref, base_ref, gate_ref,
    scaled, product, late_gate, spectrum, late_spectrum,
):
    total = HEAD + mid_ref.shape[0]
    rows = total - EDGE

    def read(at, lanes):
        if at < HEAD:
            return head_ref[at : at + STEP, lanes].astype(F32)
        return mid_ref[at - HEAD : at - HEAD + STEP, lanes].astype(F32)

    def inverse(at):
        if at < HEAD:
            return head_inv_ref[at : at + STEP, :]
        return inv_ref[at - HEAD : at - HEAD + STEP, :]

    def streams(tile):
        for half in range(WIDE // LANES):
            lanes = pl.ds(tile * WIDE + half * LANES, LANES)
            column = scaled.at[tile * 2 + half]
            taps = tap_rows(gain_ref[0, 1:2, lanes], feat_ref, lanes)
            for at in range(0, total, STEP):
                column[at : at + STEP, :] = read(at, lanes) * inverse(at)
            for at in range(0, rows, STEP):
                k = three_taps(column, EDGE + at, taps[1])
                v = three_taps(column, EDGE + at, taps[2])
                w = (k * v).astype(BF16)
                product[at : at + STEP, lanes] = w
                q = three_taps(column, EDGE + at, taps[0])
                if at < REACH:
                    gate_ref[at : at + STEP, lanes] = q
                else:
                    late_gate[at - REACH : at - REACH + STEP, lanes] = q

    def spectra(tile):
        lanes = pl.ds(tile * WIDE, WIDE)
        early = jnp.dot(
            forward_ref[:, REACH:], product[0:REACH, lanes], preferred_element_type=F32
        )
        multiply_spectra(early, table_ref, spectrum, lanes)
        late = jnp.dot(
            forward_ref[:, 0:rows], product[:, lanes], preferred_element_type=F32
        )
        multiply_spectra(late, table_ref, late_spectrum, lanes)

    def results(tile):
        lanes = pl.ds(tile * WIDE, WIDE)
        first = jnp.dot(
            backward_ref[REACH:, :], spectrum[:, lanes], preferred_element_type=F32
        )
        for at in range(0, REACH, STEP):
            base_ref[at : at + STEP, lanes] = (
                read(EDGE + at, lanes)
                + gate_ref[at : at + STEP, lanes] * first[at : at + STEP]
            )
        last = jnp.dot(
            backward_ref[REACH:rows, :],
            late_spectrum[:, lanes],
            preferred_element_type=F32,
        )
        for at in range(0, rows - REACH, STEP):
            out_ref[at : at + STEP, lanes] = (
                read(EDGE + REACH + at, lanes)
                + late_gate[at : at + STEP, lanes] * last[at : at + STEP]
            ).astype(BF16)

    staggered(mid_ref.shape[1] // WIDE, streams, spectra, results)


def halo_kernel(
    main_ref, stat_ref, gain_ref, feat_first_ref, se_ref, feat_ref, table_ref,
    forward_ref, backward_ref, base_ref, gate_ref, held_ref,
    out_ref,
    first_inv, second_inv, scaled, se_product, again, product, spectrum,
    *, start,
):
    del held_ref
    columns = scaled.shape[0]

    @pl.when(pl.program_id(0) == 0)
    def _():
        shown = jnp.where(first_block(), 0.0, 1.0)
        for i, inverse in enumerate((first_inv, second_inv)):
            row = jnp.zeros((1, WIDE), F32)
            for k in range(PIECES):
                lanes = pl.ds((i * PIECES + k) * WIDE, WIDE)
                row = row + stat_ref[0:STEP, lanes].astype(F32)[0:1]
            column = to_column(row * shown, start, HALO)
            inverse[...] = jnp.broadcast_to(column, inverse.shape)
        scaled[:, 0:PAD, :] = jnp.zeros((columns, PAD, LANES), F32)
        se_product[:, 0:PAD, :] = jnp.zeros((columns, PAD, LANES), F32)

    def read(at, lanes):
        return main_ref[at : at + STEP, lanes].astype(F32)

    def streams(tile):
        for half in range(WIDE // LANES):
            lanes = pl.ds(tile * WIDE + half * LANES, LANES)
            column = scaled.at[tile * 2 + half]
            se_column = se_product.at[tile * 2 + half]
            late_column = again.at[tile * 2 + half]
            taps = tap_rows(gain_ref[0, 0:1, lanes], feat_first_ref, lanes)
            filter_taps = [se_ref[0, i : i + 1, lanes] for i in range(7)]
            late_taps = tap_rows(gain_ref[0, 1:2, lanes], feat_ref, lanes)
            for at in range(0, HALO, STEP):
                column[PAD + at : PAD + at + STEP, :] = (
                    read(at, lanes) * first_inv[at : at + STEP, :]
                )
            for at in range(0, HALO, STEP):
                k = three_taps(column, PAD + at, taps[1])
                v = three_taps(column, PAD + at, taps[2])
                se_column[PAD + at : PAD + at + STEP, :] = (
                    (k * v).astype(BF16).astype(F32)
                )
            for at in range(0, HALO, STEP):
                q = three_taps(column, PAD + at, taps[0])
                f = se_filter(se_column, PAD + at, filter_taps)
                result = (read(at, lanes) + q * f).astype(BF16).astype(F32)
                late_column[at : at + STEP, :] = result * second_inv[at : at + STEP, :]
            for at in range(HALO - REACH, HALO, STEP):
                k = three_taps(late_column, at, late_taps[1])
                v = three_taps(late_column, at, late_taps[2])
                to = at - (HALO - REACH)
                product[to : to + STEP, lanes] = (k * v).astype(BF16)

    def spectra(tile):
        halo_spectra(tile, product, forward_ref, table_ref, spectrum)

    def results(tile):
        halo_results(tile, spectrum, backward_ref, base_ref, gate_ref, out_ref)

    staggered(main_ref.shape[1] // WIDE, streams, spectra, results)


def halo_spectra(tile, product, forward_ref, table_ref, spectrum):
    lanes = pl.ds(tile * WIDE, WIDE)
    seen = jnp.dot(
        forward_ref[:, 0:REACH], product[:, lanes], preferred_element_type=F32
    )
    multiply_spectra(seen, table_ref, spectrum, lanes)


def halo_results(
    tile, spectrum, backward_ref, base_ref, gate_ref, out_ref, shown=None
):
    lanes = pl.ds(tile * WIDE, WIDE)
    carried = jnp.dot(
        backward_ref[REACH:, :], spectrum[:, lanes], preferred_element_type=F32
    )
    for at in range(0, REACH, STEP):
        gate = gate_ref[at : at + STEP, lanes]
        if shown is not None:
            gate = gate * shown
        out_ref[at : at + STEP, lanes] = (
            base_ref[at : at + STEP, lanes] + gate * carried[at : at + STEP]
        ).astype(BF16)


def tail_kernel(
    tail_ref, table_ref, forward_ref, backward_ref, base_ref, gate_ref, held_ref,
    out_ref,
    spectrum,
):
    del held_ref
    shown = jnp.where(first_block(), 0.0, 1.0)

    def spectra(tile):
        halo_spectra(tile, tail_ref, forward_ref, table_ref, spectrum)

    def results(tile):
        halo_results(tile, spectrum, backward_ref, base_ref, gate_ref, out_ref, shown)

    staggered(tail_ref.shape[1] // WIDE, spectra, results)


def whole(array):
    return pl.BlockSpec(array.shape, lambda *_: (0,) * array.ndim)


def on_device(tokens, norm_gain, feat_taps, se_taps, mr_taps):
    rows, width = tokens.shape
    total = rows + EDGE
    forward, backward, late_forward = transform_tables()
    length = lax.axis_size(("section", "ctx"))

    def from_behind(x):
        pairs = [(i, (i + 1) % length) for i in range(length)]
        return lax.ppermute(x, ("section", "ctx"), pairs)

    def place(i):
        return i // RING, i % RING

    def backward_hop(x):
        pairs = []
        for i in range(length):
            line, z = place(i)
            pairs.append((i, line * RING + (z - 1) % RING))
        return lax.ppermute(x, ("section", "ctx"), pairs)

    def last_hop(x):
        pairs = []
        for i in range(length):
            line, z = place(i)
            pairs.append((line * RING + (z - 2) % RING, (i + 1) % length))
        return lax.ppermute(x, ("section", "ctx"), pairs)

    parts = EARLY[0] // EARLY[1]
    early, around = pl.pallas_call(
        gather_kernel,
        in_specs=[pl.BlockSpec(memory_space=pl.ANY)],
        out_specs=[pl.BlockSpec(memory_space=pl.ANY)] * 2,
        out_shape=[
            jax.ShapeDtypeStruct((HALO + EDGE * parts, EARLY[1]), BF16),
            jax.ShapeDtypeStruct((HALO, ROUND[1]), BF16),
        ],
        scratch_shapes=[pltpu.SemaphoreType.DMA((2 + parts,))],
        compiler_params=params(),
        cost_estimate=cost(1),
        name="gather",
    )(tokens)
    around = backward_hop(around)
    early = from_behind(early)

    groups = 2048 // 16
    table = pl.pallas_call(
        taps_transform_kernel,
        grid=(width // 2048,),
        in_specs=[
            pl.BlockSpec((REACH, groups), lambda j: (0, j)),
            pl.BlockSpec((POINTS, REACH), lambda j: (0, 0)),
        ],
        out_specs=pl.BlockSpec((POINTS, 2048), lambda j: (0, j)),
        out_shape=jax.ShapeDtypeStruct((POINTS, width), BF16),
        scratch_shapes=[pltpu.VMEM((groups, 2048), BF16)],
        compiler_params=params(),
        cost_estimate=cost(2.5),
        name="taps_transform",
    )(mr_taps[0], forward)

    se_specs = [
        whole(norm_gain),
        pl.BlockSpec((1, 1, 3, 3, width), lambda i: (0, 0, 0, 0, 0)),
        whole(se_taps),
    ]

    def se_scratch(height, slots):
        return [
            pltpu.VMEM((height, LANES), F32),
            pltpu.VMEM((height, LANES), F32),
            pltpu.VMEM((slots, PAD + height, LANES), F32),
            pltpu.VMEM((slots, PAD + height, LANES), F32),
        ]

    def all_of(*shape):
        return pl.BlockSpec(shape, lambda *_: (0,) * len(shape))

    mid_rows = rows - EDGE
    mid, inv, *tails = pl.pallas_call(
        own_se_kernel,
        grid=(1,),
        in_specs=[
            whole(tokens),
            *se_specs,
            pl.BlockSpec((1, 1, 3, 3, width), lambda i: (0, 1, 0, 0, 0)),
        ],
        out_specs=[all_of(mid_rows, width), all_of(mid_rows, LANES)]
        + [all_of(REACH, size) for _, size in LATE],
        out_shape=[
            jax.ShapeDtypeStruct((mid_rows, width), BF16),
            jax.ShapeDtypeStruct((mid_rows, LANES), F32),
        ]
        + [jax.ShapeDtypeStruct((REACH, size), BF16) for _, size in LATE],
        scratch_shapes=se_scratch(rows, 1),
        compiler_params=params(),
        cost_estimate=cost(14),
        name="own_se",
    )(tokens, norm_gain, feat_taps, se_taps, feat_taps)
    tails[0] = from_behind(tails[0])
    around, mid = lax.optimization_barrier((around, mid))
    around = backward_hop(around)

    head, head_inv = pl.pallas_call(
        head_se_kernel,
        grid=(1,),
        in_specs=[all_of(EDGE, width), whole(early), *se_specs],
        out_specs=[all_of(HEAD, width), all_of(HEAD, LANES)],
        out_shape=[
            jax.ShapeDtypeStruct((HEAD, width), BF16),
            jax.ShapeDtypeStruct((HEAD, LANES), F32),
        ],
        scratch_shapes=se_scratch(HEAD, 4),
        compiler_params=params(),
        cost_estimate=cost(3),
        name="head_se",
    )(tokens, early, norm_gain, feat_taps, se_taps)

    head, table, *later = lax.optimization_barrier((head, table, *tails[1:]))
    tails[1:] = [from_behind(tail) for tail in later]
    around, head = lax.optimization_barrier((around, head))
    around = last_hop(around)

    def feat_spec(block, which, first):
        return pl.BlockSpec((1, 1, 3, 3, block), lambda j: (0, which, 0, 0, first + j))

    def columns(height, block, first=0, row=0):
        return pl.BlockSpec((height, block), lambda j: (row, first + j))

    block = OWN_BLOCK
    out, base, gate = pl.pallas_call(
        own_mr_kernel,
        grid=(width // block,),
        in_specs=[
            columns(HEAD, block),
            columns(mid_rows, block),
            whole(head_inv),
            whole(inv),
            pl.BlockSpec((1, 2, block), lambda j: (0, 0, j)),
            feat_spec(block, 1, 0),
            columns(POINTS, block),
            whole(forward),
            whole(backward),
        ],
        out_specs=[
            columns(rows - REACH, block, 0, REACH // (rows - REACH)),
            columns(REACH, block),
            columns(REACH, block),
        ],
        out_shape=[
            jax.ShapeDtypeStruct((rows, width), BF16),
            jax.ShapeDtypeStruct((REACH, width), F32),
            jax.ShapeDtypeStruct((REACH, width), F32),
        ],
        scratch_shapes=[
            pltpu.VMEM((block // LANES, rows + EDGE, LANES), F32),
            pltpu.VMEM((rows, block), BF16),
            pltpu.VMEM((rows - REACH, block), F32),
            pltpu.VMEM((POINTS, block), BF16),
            pltpu.VMEM((POINTS, block), BF16),
        ],
        compiler_params=params(),
        cost_estimate=cost(12),
        name="own_mr",
    )(head, mid, head_inv, inv, norm_gain, feat_taps, table, forward, backward)

    block = HALO_BLOCK
    for (start, size), main in ((EARLY, early), (ROUND, around)):
        first = start // block
        out = pl.pallas_call(
            functools.partial(halo_kernel, start=mid_rows - HALO),
            grid=(size // block,),
            in_specs=[
                columns(HALO, block),
                all_of(STEP, 2 * PIECES * WIDE),
                pl.BlockSpec((1, 2, block), lambda j: (0, 0, first + j)),
                feat_spec(block, 0, first),
                pl.BlockSpec((1, 7, block), lambda j: (0, 0, first + j)),
                feat_spec(block, 1, first),
                columns(POINTS, block, first),
                whole(forward),
                whole(backward),
                columns(REACH, block, first),
                columns(REACH, block, first),
                pl.BlockSpec(memory_space=pl.ANY),
            ],
            out_specs=columns(REACH, block, first),
            out_shape=jax.ShapeDtypeStruct((rows, width), BF16),
            input_output_aliases={11: 0},
            scratch_shapes=[
                pltpu.VMEM((HALO, LANES), F32),
                pltpu.VMEM((HALO, LANES), F32),
                pltpu.VMEM((block // LANES, PAD + HALO, LANES), F32),
                pltpu.VMEM((block // LANES, PAD + HALO, LANES), F32),
                pltpu.VMEM((block // LANES, HALO, LANES), F32),
                pltpu.VMEM((REACH, block), BF16),
                pltpu.VMEM((POINTS, block), BF16),
            ],
            compiler_params=params(),
            cost_estimate=cost(6),
            name="halo",
        )(
            main, tails[0], norm_gain, feat_taps, se_taps, feat_taps, table,
            forward, backward, base, gate, out,
        )

    for (start, size), tail in zip(LATE, tails):
        block = TAIL_BLOCK
        out = pl.pallas_call(
            tail_kernel,
            grid=(size // block,),
            in_specs=[
                columns(REACH, block),
                columns(POINTS, block, start // block),
                whole(late_forward),
                whole(backward),
                columns(REACH, block, start // block),
                columns(REACH, block, start // block),
                pl.BlockSpec(memory_space=pl.ANY),
            ],
            out_specs=columns(REACH, block, start // block),
            out_shape=jax.ShapeDtypeStruct((rows, width), BF16),
            input_output_aliases={6: 0},
            scratch_shapes=[
                pltpu.VMEM((POINTS, block), BF16),
            ],
            compiler_params=params(),
            cost_estimate=cost(3),
        name="tail",
        )(tail, table, late_forward, backward, base, gate, out)
    return out


def solution(mesh):
    placed = (P(("section", "ctx"), None), P(), P(), P(), P())
    return jax.shard_map(
        on_device,
        mesh=mesh,
        in_specs=placed,
        out_specs=P(("section", "ctx"), None),
        check_vma=False,
    )
```
